32 devices in a mesh: dp: 2 (over x), expert: 16 (over z, y, core).
Axes of the slice: x: 2, y: 2, z: 4, core: 2. Of those that a mesh axis runs over, the one named last changes fastest.
Arguments:
- query_reps: bfloat16 [256, 2048], P('dp'), as said below
- code_reps: bfloat16 [256, 2048], P('expert'), as said below
- positives: int32 [256], P('dp'), may hold values from 0 to 255, as said below
- file_lengths: int32 [16, 2, 8], P('expert', 'dp'), may hold values from 1 to 64, 128 in all within a row
- residual: bfloat16 [16, 256, 2048], P('expert', 'dp'), may hold values from -6 to 6
- norm_gain: bfloat16 [2048], replicated, may hold values from 0.25 to 1.75
- expert_ids: int32 [16, 256, 2], P('expert', 'dp'), may hold values from 0 to 15, as said below
- gate_units: int32 [16, 256, 2], P('expert', 'dp'), may hold values from 16 to 191
- w_gate: bfloat16 [16, 2048, 768], P('expert', 'dp'), may hold values from -0.125 to 0.125
- w_up: bfloat16 [16, 2048, 768], P('expert', 'dp'), may hold values from -0.125 to 0.125
- w_down: bfloat16 [16, 2048, 768], P('expert', 'dp'), may hold values from -0.21875 to 0.21875
Outputs:
- token_grad: bfloat16 [16, 256, 2048], P('expert', 'dp')
The draws below stay inside these ranges and needn't reach their ends.
Inputs may be any that keep to these rules, and one draw needn't show every extreme that they name: `positives`: each code is the positive of exactly one query. `query_reps`: entries have magnitude at most 4 / sqrt(2048). `code_reps`: entries have magnitude at most 4 / sqrt(2048). `file_lengths`: the 8 lengths of one shard add up to 128. `expert_ids`: each token names 2 different experts; the tokens of one shard name each expert at most 24 times, and for each index of dp some expert is named exactly 24 times by the tokens of every shard with that index.
All inputs are finite; a program needn't handle non-finite values.
Results may differ from the reference program's by a relative error of at most 0.009.
Values may be sent and summed in bfloat16 or wider, within the bound.
A program may use at most 64 MiB of HBM per device.

```python
import math
import jax
import jax.numpy as jnp
import numpy as np
from jax import lax

D = 2048
FF = 768
TOK_DEV = 128
TOP = 2
EXPERTS = 16
SHARDS = 2
FILES_DEV = 8
MOSTLEN = 64
CAP = 24
FILES = 256


RHO = 0.45


NOISE_WEIGHT = 0.89


def shared_reps(key):
    file_total = FILES
    spread = D ** (-0.5)
    key_pos = jax.random.fold_in(key, 11)
    key_code = jax.random.fold_in(key, 12)
    key_noise = jax.random.fold_in(key, 13)
    positives = jax.random.permutation(key_pos, file_total).astype(jnp.int32)
    codes = jax.random.truncated_normal(key_code, -3.0, 3.0, (file_total, D), jnp.float32)
    noise = jax.random.truncated_normal(key_noise, -3.0, 3.0, (file_total, D), jnp.float32)
    queries = RHO * codes[positives] + NOISE_WEIGHT * noise
    codes = jnp.clip(codes, -4.0, 4.0) * spread
    queries = jnp.clip(queries, -4.0, 4.0) * spread
    return (positives, codes, queries)


def draw_positives(key, part):
    return shared_reps(key)[0]


def draw_code_reps(key, part):
    return shared_reps(key)[1].astype(jnp.bfloat16)


def draw_query_reps(key, part):
    return shared_reps(key)[2].astype(jnp.bfloat16)


def draw_expert_ids(key, part):
    slot_total = EXPERTS * CAP
    hot_expert = jax.random.randint(jax.random.fold_in(key, 21), (SHARDS,), 0, EXPERTS)

    def one_block(block):
        block_key = jax.random.fold_in(key, 1000 + block)
        key_score = jax.random.fold_in(block_key, 1)
        key_perm = jax.random.fold_in(block_key, 2)
        number = jnp.arange(slot_total, dtype=jnp.int32)
        slot_owner = number // CAP
        scores = jax.random.randint(key_score, (slot_total,), 0, 262144) * slot_total + number
        scores = jnp.where(slot_owner == hot_expert[block % SHARDS], number - slot_total, scores)
        ranking = jnp.argsort(scores)
        picked = jnp.sort(ranking[:TOK_DEV * TOP])
        pairs = (picked // CAP).reshape(TOP, TOK_DEV).T
        return pairs[jax.random.permutation(key_perm, TOK_DEV)]
    blocks = jax.vmap(one_block)(jnp.arange(EXPERTS * SHARDS, dtype=jnp.int32))
    return blocks.reshape(EXPERTS, SHARDS * TOK_DEV, TOP).astype(jnp.int32)


def with_ends(drawn, key, low, high):
    longest = drawn.shape.index(max(drawn.shape))
    spots = []
    for shift in (0, 1):
        where = [jax.random.randint(jax.random.fold_in(key, axis), (), 0, length) for axis, length in enumerate(drawn.shape)]
        where[longest] = (where[longest] + shift) % drawn.shape[longest]
        spots.append(tuple(where))
    return drawn.at[spots[0]].set(low).at[spots[1]].set(high)


def block_levels(stream_key, extent, pieces, low, top_value):
    level = 1.0
    for dim, blocks in pieces:
        heights = jax.random.uniform(jax.random.fold_in(jax.random.fold_in(stream_key, 6), dim), (blocks,), jnp.float32, low / len(pieces), top_value / len(pieces))
        level = level * jnp.repeat(jnp.exp(heights), extent[dim] // blocks).reshape((-1,) + (1,) * (len(extent) - 1 - dim))
    return level


def profile(count, total, bound, skew):
    portions = [(1 << 20) // math.isqrt(grade ** skew) + 1 for grade in range(2, count + 1)]
    surplus, holding = total - bound - (count - 1), [1] * (count - 1)
    while surplus > 0:
        free = [i for i in range(count - 1) if holding[i] < bound]
        whole, budget = sum([portions[i] for i in free]), surplus
        for i in free:
            more = min(bound - holding[i], max(1, budget * portions[i] // whole), surplus)
            holding[i] = holding[i] + more
            surplus = surplus - more
    return np.array([bound] + holding)


def ragged_sizes(own_key, number_of, total, limit, lean):
    if number_of == 2:
        one = jax.random.randint(own_key, (), max(1, total - limit), min(limit, total - 1) + 1)
        return jnp.stack([one, total - one])
    sizes = jnp.asarray(profile(number_of, total, limit, lean), jnp.int32)
    twos = (number_of - 1) // 2
    donor, taker = sizes[1:1 + 2 * twos:2], sizes[2:2 + 2 * twos:2]
    margin = jnp.minimum(donor - 1, limit - taker)
    passed = jax.random.randint(jax.random.fold_in(own_key, 1), (twos,), 0, 1 << 20) % (margin + 1)
    sizes = sizes.at[1:1 + 2 * twos:2].set(donor - passed).at[2:2 + 2 * twos:2].set(taker + passed)
    return sizes[jax.random.permutation(jax.random.fold_in(own_key, 2), number_of)]


def gaussian(rng, extent, scale, most, cuts=(), held_as=jnp.bfloat16):
    gain = block_levels(rng, extent, cuts, -0.22, 0.18) if cuts else 1.0
    drawn = jax.random.normal(rng, extent, jnp.float32) * scale * gain
    return jnp.minimum(jnp.maximum(drawn, -most), most).astype(held_as)


def setup_inputs(seed: int = 0) -> dict:
    splits = jax.random.split(jax.random.key(seed), 12)
    return {
        "query_reps": draw_query_reps(jax.random.fold_in(splits[11], 71), 0),
        "code_reps": draw_code_reps(jax.random.fold_in(splits[11], 71), 0),
        "positives": draw_positives(jax.random.fold_in(splits[11], 71), 0),
        "file_lengths": jax.vmap(lambda own: ragged_sizes(own, FILES_DEV, TOK_DEV, MOSTLEN, 2))(jax.random.split(splits[3], EXPERTS * SHARDS)).reshape((EXPERTS, SHARDS, FILES_DEV)).astype(jnp.int32),
        "residual": gaussian(splits[4], (EXPERTS, SHARDS * TOK_DEV, D), 1.0, 6.0, ((0, 16), (1, 2))),
        "norm_gain": jnp.clip(1.0 + 0.15 * jax.random.normal(splits[5], (D,), jnp.float32), 0.25, 1.75).astype(jnp.bfloat16),
        "expert_ids": draw_expert_ids(jax.random.fold_in(splits[11], 71), 0),
        "gate_units": with_ends(jax.random.randint(splits[7], (EXPERTS, SHARDS * TOK_DEV, TOP), 16, 192), jax.random.fold_in(splits[7], 1), 16, 191).astype(jnp.int32),
        "w_gate": gaussian(splits[8], (EXPERTS, D, FF), D ** -0.5, 0.125, ((0, 16), (1, 2))),
        "w_up": gaussian(splits[9], (EXPERTS, D, FF), D ** -0.5, 0.125, ((0, 16), (1, 2))),
        "w_down": gaussian(splits[10], (EXPERTS, D, FF), FF ** -0.5, 0.21875, ((0, 16), (1, 2))),
    }


SCORE_SCALE = 20.0
GRAD_SCALE = 2560.0
EPSILON = 1e-06

def expert_backward(normed_rows, cot_rows, gate_rows, weight_gate, weight_up, weight_down):
    gate_pre = jnp.dot(normed_rows, weight_gate, preferred_element_type=jnp.float32)
    up_pre = jnp.dot(normed_rows, weight_up, preferred_element_type=jnp.float32)
    back_hidden = gate_rows[:, None] * jnp.dot(cot_rows, weight_down, preferred_element_type=jnp.float32)
    sigmoid_gate = jax.nn.sigmoid(gate_pre)
    grad_gate = (back_hidden * up_pre * sigmoid_gate * (1.0 + gate_pre * (1.0 - sigmoid_gate))).astype(jnp.bfloat16)
    grad_up = (back_hidden * gate_pre * sigmoid_gate).astype(jnp.bfloat16)
    contract = (((1,), (1,)), ((), ()))
    input_grad = lax.dot_general(grad_gate, weight_gate, contract, preferred_element_type=jnp.float32)
    input_grad = input_grad + lax.dot_general(grad_up, weight_up, contract, preferred_element_type=jnp.float32)
    return input_grad.astype(jnp.bfloat16)

def reference(query_reps, code_reps, positives, file_lengths, residual, norm_gain, expert_ids, gate_units, w_gate, w_up, w_down):
    file_total = query_reps.shape[0]
    scores = jnp.dot(query_reps, code_reps.T, preferred_element_type=jnp.float32) * SCORE_SCALE
    row_top = lax.optimization_barrier(jnp.max(scores, axis=1, keepdims=True))
    exponent = jnp.exp(scores - row_top)
    probabilities = exponent / lax.optimization_barrier(jnp.sum(exponent, axis=1, keepdims=True))
    onehot = (positives[:, None] == jnp.arange(file_total, dtype=jnp.int32)[None, :]).astype(jnp.float32)
    weights = (GRAD_SCALE * (probabilities - onehot)).astype(jnp.bfloat16)
    code_grad = jnp.dot(weights.T, query_reps, preferred_element_type=jnp.float32)
    owners, seq_rows, model_width = residual.shape
    shard_count = file_lengths.shape[1]
    file_count = file_lengths.shape[2]
    tokens = seq_rows // shard_count
    lengths = file_lengths.astype(jnp.float32)
    file_cot = (code_grad.reshape(owners, shard_count, file_count, model_width) / lengths[..., None]).astype(jnp.bfloat16)
    file_ends = jnp.cumsum(file_lengths, axis=2).astype(jnp.int32)
    position = jnp.arange(tokens, dtype=jnp.int32)
    segment = lax.optimization_barrier(jnp.sum((position[None, None, :, None] >= file_ends[:, :, None, :]).astype(jnp.int32), axis=3)).astype(jnp.int32)
    block_base = jnp.arange(owners * shard_count, dtype=jnp.int32).reshape(owners, shard_count) * file_count
    file_index = (block_base[:, :, None] + segment).reshape(-1)
    token_cot = file_cot.reshape(-1, model_width)[file_index]
    stream = residual.astype(jnp.float32)
    root_inverse = lax.rsqrt(lax.optimization_barrier(jnp.mean(stream * stream, axis=-1, keepdims=True)) + EPSILON)
    norm_scale = norm_gain.astype(jnp.float32)
    normed = (stream * root_inverse * norm_scale).astype(jnp.bfloat16)
    token_count = owners * seq_rows
    flat_normed = normed.reshape(token_count, model_width)
    flat_ids = expert_ids.reshape(-1).astype(jnp.int32)
    gate_values = gate_units.reshape(-1).astype(jnp.float32) / 256.0
    count_total = flat_ids.shape[0]
    ranking = jnp.argsort(flat_ids, stable=True).astype(jnp.int32)
    counts = lax.optimization_barrier(jnp.sum((flat_ids[None, :] == jnp.arange(owners, dtype=jnp.int32)[:, None]).astype(jnp.int32), axis=1)).astype(jnp.int32)
    starts = (jnp.cumsum(counts) - counts).astype(jnp.int32)
    row_bound = CAP * SHARDS * EXPERTS
    padded_order = jnp.concatenate([ranking, jnp.full((row_bound,), count_total, jnp.int32)])
    normed_pad = jnp.concatenate([flat_normed, jnp.zeros((1, model_width), jnp.bfloat16)])
    cot_pad = jnp.concatenate([token_cot, jnp.zeros((1, model_width), jnp.bfloat16)])
    gate_pad = jnp.concatenate([gate_values, jnp.zeros((1,), jnp.float32)])

    def one_expert(carry, expert):
        picked = lax.dynamic_slice_in_dim(padded_order, starts[expert], row_bound)
        is_valid = jnp.arange(row_bound, dtype=jnp.int32) < counts[expert]
        picked = jnp.where(is_valid, picked, count_total).astype(jnp.int32)
        token_row = jnp.where(is_valid, picked // TOP, token_count).astype(jnp.int32)
        input_grad = expert_backward(normed_pad[token_row], cot_pad[token_row], gate_pad[picked], w_gate[expert], w_up[expert], w_down[expert])
        return (carry.at[token_row].add(input_grad.astype(jnp.float32)), None)
    normed_grad, _ = lax.scan(one_expert, jnp.zeros((token_count + 1, model_width), jnp.float32), jnp.arange(owners, dtype=jnp.int32))
    normed_grad = normed_grad[:token_count].reshape(owners, seq_rows, model_width)
    scaled = norm_scale * normed_grad
    correction = lax.optimization_barrier(jnp.mean(scaled * stream, axis=-1, keepdims=True))
    token_grad = token_cot.reshape(owners, seq_rows, model_width).astype(jnp.float32) + root_inverse * scaled - stream * root_inverse ** 3 * correction
    return token_grad.astype(jnp.bfloat16)
```

```python
import functools

import jax
import jax.numpy as jnp
from jax import lax
from jax.experimental import pallas as pl
from jax.experimental.pallas import tpu as pltpu
from jax.sharding import PartitionSpec as P

SCORE_SCALE = 20.0
GRAD_SCALE = 2560.0
EPSILON = 1e-06


def joined(value, axis, join):
    pieces = jax.tree.map(lambda part: lax.all_gather(part, axis), value)
    head = jax.tree.map(lambda part: part[0], pieces)
    tail = jax.tree.map(lambda part: part[1:], pieces)
    subtotal, _ = lax.scan(lambda subtotal, slab: (join(subtotal, slab), None), head, tail)
    return subtotal


def softmax_pair(first, second):
    row_top = jnp.maximum(first[0], second[0])
    return (
        row_top,
        first[1] * jnp.exp(first[0] - row_top) + second[1] * jnp.exp(second[0] - row_top),
    )


def expert_backward(normed_rows, cot_rows, gate_rows, weight_gate, weight_up, weight_down):
    gate_pre = jnp.dot(normed_rows, weight_gate, preferred_element_type=jnp.float32)
    up_pre = jnp.dot(normed_rows, weight_up, preferred_element_type=jnp.float32)
    back_hidden = gate_rows[:, None] * jnp.dot(
        cot_rows, weight_down, preferred_element_type=jnp.float32
    )
    sigmoid_gate = jax.nn.sigmoid(gate_pre)
    grad_gate = (
        back_hidden * up_pre * sigmoid_gate * (1.0 + gate_pre * (1.0 - sigmoid_gate))
    ).astype(jnp.bfloat16)
    grad_up = (back_hidden * gate_pre * sigmoid_gate).astype(jnp.bfloat16)
    contract = (((1,), (1,)), ((), ()))
    input_grad = lax.dot_general(
        grad_gate, weight_gate, contract, preferred_element_type=jnp.float32
    )
    input_grad = input_grad + lax.dot_general(
        grad_up, weight_up, contract, preferred_element_type=jnp.float32
    )
    return input_grad.astype(jnp.bfloat16)


def collective_plan(
    query_reps,
    code_reps,
    positives,
    file_lengths,
    residual,
    norm_gain,
    expert_ids,
    gate_units,
    w_gate,
    w_up,
    w_down,
):
    owners = lax.axis_size("expert")
    columns = code_reps.shape[0]
    file_count = file_lengths.shape[2]
    tokens = residual.shape[1]
    model_width = residual.shape[2]
    pick_count = expert_ids.shape[2]
    capacity = 3 * tokens * pick_count // (2 * owners)
    scores = jnp.dot(query_reps, code_reps.T, preferred_element_type=jnp.float32) * SCORE_SCALE
    local_top = jnp.max(scores, axis=1)
    local_total = jnp.sum(jnp.exp(scores - local_top[:, None]), axis=1)
    row_top, row_total = joined((local_top, local_total), "expert", softmax_pair)
    probabilities = jnp.exp(scores - row_top[:, None]) / row_total[:, None]
    column_ids = lax.axis_index("expert") * columns + jnp.arange(columns, dtype=jnp.int32)
    onehot = (positives[:, None] == column_ids[None, :]).astype(jnp.float32)
    weights = (GRAD_SCALE * (probabilities - onehot)).astype(jnp.bfloat16)
    code_grad = lax.psum_scatter(
        lax.dot_general(
            weights, query_reps, (((0,), (0,)), ((), ())), preferred_element_type=jnp.float32
        ),
        "dp",
        scatter_dimension=0,
        tiled=True,
    )
    lengths = file_lengths[0, 0]
    file_cot = (code_grad / lengths[:, None].astype(jnp.float32)).astype(jnp.bfloat16)
    file_ends = jnp.cumsum(lengths)
    position = jnp.arange(tokens, dtype=jnp.int32)
    segment = jnp.sum((position[:, None] >= file_ends[None, :]).astype(jnp.int32), axis=1)
    member = (segment[:, None] == jnp.arange(file_count, dtype=jnp.int32)[None, :]).astype(
        jnp.bfloat16
    )
    token_cot = jnp.dot(member, file_cot, preferred_element_type=jnp.float32).astype(jnp.bfloat16)
    stream = residual[0].astype(jnp.float32)
    root_inverse = lax.rsqrt(jnp.mean(stream * stream, axis=-1, keepdims=True) + EPSILON)
    norm_scale = norm_gain.astype(jnp.float32)
    normed = (stream * root_inverse * norm_scale).astype(jnp.bfloat16)
    chosen = expert_ids[0].reshape(-1)
    gate_values = gate_units[0].reshape(-1)
    assign_count = chosen.shape[0]
    expert_table = (chosen[:, None] == jnp.arange(owners, dtype=jnp.int32)[None, :]).astype(
        jnp.int32
    )
    earlier = jnp.cumsum(expert_table, axis=0) - expert_table
    slot_rank = jnp.sum(earlier * expert_table, axis=1)
    slot_index = chosen * capacity + slot_rank
    source = (
        jnp.full((owners * capacity,), assign_count, jnp.int32)
        .at[slot_index]
        .set(jnp.arange(assign_count, dtype=jnp.int32))
    )
    filled = source < assign_count
    token_of = jnp.where(filled, source // pick_count, tokens)
    gate_pad = jnp.concatenate(
        [gate_values.astype(jnp.float32) / 256.0, jnp.zeros((1,), jnp.float32)]
    )
    send_gate = gate_pad[source].astype(jnp.bfloat16).reshape(owners, capacity)
    normed_pad = jnp.concatenate([normed, jnp.zeros((1, model_width), jnp.bfloat16)])
    send_rows = normed_pad[token_of].reshape(owners, capacity, model_width)
    gathered = (
        lax.all_gather(w_gate, "dp", axis=1, tiled=True),
        lax.all_gather(w_up, "dp", axis=1, tiled=True),
        lax.all_gather(w_down, "dp", axis=1, tiled=True),
    )
    weight_gate = gathered[0][0]
    weight_up = gathered[1][0]
    weight_down = gathered[2][0]
    cot_pad = jnp.concatenate([token_cot, jnp.zeros((1, model_width), jnp.bfloat16)])
    send_cot = cot_pad[token_of].reshape(owners, capacity, model_width)
    row_block = lax.all_to_all(send_rows, "expert", split_axis=0, concat_axis=0, tiled=True)
    cot_block = lax.all_to_all(send_cot, "expert", split_axis=0, concat_axis=0, tiled=True)
    gate_rows = lax.all_to_all(send_gate, "expert", split_axis=0, concat_axis=0, tiled=True)
    senders = gate_rows.shape[0]
    items = gate_rows.shape[1]
    input_grad = expert_backward(
        row_block.reshape(-1, model_width),
        cot_block.reshape(-1, model_width),
        gate_rows.reshape(-1).astype(jnp.float32),
        weight_gate,
        weight_up,
        weight_down,
    )
    result = input_grad.reshape(senders, items, model_width)
    returned = lax.all_to_all(result, "expert", split_axis=0, concat_axis=0, tiled=True)
    per_pick = returned.reshape(owners * capacity, model_width)[slot_index].astype(jnp.float32)
    normed_grad = jnp.sum(per_pick.reshape(tokens, pick_count, model_width), axis=1)
    scaled = norm_scale * normed_grad
    correction = jnp.mean(scaled * stream, axis=-1, keepdims=True)
    token_grad = (
        token_cot.astype(jnp.float32)
        + root_inverse * scaled
        - stream * root_inverse**3 * correction
    )
    return token_grad.astype(jnp.bfloat16)[None]


MESH = pl.DeviceIdType.MESH
CONTRACT_LAST = (((1,), (1,)), ((), ()))


def matmul(left, right):
    return jnp.dot(left, right, preferred_element_type=jnp.float32)


def matmul_t(left, right):
    return lax.dot_general(left, right, CONTRACT_LAST, preferred_element_type=jnp.float32)


def iota(shape, axis):
    return lax.broadcasted_iota(jnp.int32, shape, axis)


def fused_kernel(
    owners,
    lengths_ref,
    query_ref,
    code_ref,
    positive_ref,
    residual_ref,
    gain_ref,
    ids_ref,
    units_ref,
    gate_hbm,
    up_hbm,
    down_hbm,
    out_ref,
    query_all,
    code_all,
    positive_all,
    gate_all,
    up_all,
    down_own,
    rows_out,
    rows_in,
    meta_out,
    meta_in,
    back_out,
    back_in,
    back_total,
    rows_expert,
    hidden_back,
    grad_hidden,
    grads_out,
    grads_in,
    combine,
    local_sem,
    pair_send,
    pair_recv,
    code_send,
    code_recv,
    rows_send,
    rows_recv,
    meta_send,
    meta_recv,
    grads_send,
    grads_recv,
):
    f32, bf16 = jnp.float32, jnp.bfloat16
    shard = lax.axis_index("dp")
    me = lax.axis_index("expert")
    other = 1 - shard
    tokens, width = residual_ref.shape
    half = width // 2
    columns = code_ref.shape[0]
    file_count = columns // 2
    files = columns * owners
    slots = meta_in.shape[1]
    block = 2 * slots
    ff = gate_all.shape[2]

    def partner(step):
        return lax.rem(me + step, owners)

    def pair_copy(index, source, target):
        return pltpu.make_async_remote_copy(
            src_ref=source,
            dst_ref=target,
            send_sem=pair_send.at[index],
            recv_sem=pair_recv.at[index],
            device_id=(other, me),
            device_id_type=MESH,
        )

    def group_copy(step, source, target, send, recv):
        return pltpu.make_async_remote_copy(
            src_ref=source,
            dst_ref=target,
            send_sem=send.at[step],
            recv_sem=recv.at[step],
            device_id=(shard, partner(step)),
            device_id_type=MESH,
        )

    def code_copy(step):
        return group_copy(step, code_ref, code_all.at[me], code_send, code_recv)

    def rows_copy(step):
        return group_copy(step, rows_out.at[partner(step)], rows_in.at[me], rows_send, rows_recv)

    def meta_copy(step):
        return group_copy(step, meta_out.at[partner(step)], meta_in.at[me], meta_send, meta_recv)

    def grads_copy(step):
        return group_copy(
            step, grads_out.at[partner(step)], grads_in.at[me], grads_send, grads_recv
        )

    def each_partner(action):
        def body(step, carry):
            action(step)
            return carry

        lax.fori_loop(1, owners, body, 0)

    barrier = pltpu.get_barrier_semaphore()
    pl.semaphore_signal(barrier, inc=1, device_id=(other, me), device_id_type=MESH)
    each_partner(
        lambda step: pl.semaphore_signal(
            barrier, inc=1, device_id=(shard, partner(step)), device_id_type=MESH
        )
    )
    local_down = pltpu.make_async_copy(down_hbm, down_own, local_sem.at[0])
    local_gate = pltpu.make_async_copy(gate_hbm, gate_all.at[shard], local_sem.at[1])
    local_up = pltpu.make_async_copy(up_hbm, up_all.at[shard], local_sem.at[2])
    local_down.start()
    local_gate.start()
    local_up.start()
    query_all[shard] = query_ref[...]
    code_all[me] = code_ref[...]
    positive_all[shard] = jnp.broadcast_to(positive_ref[...], (8, positive_ref.shape[1]))
    pl.semaphore_wait(barrier, owners)

    query_pair = pair_copy(0, query_ref, query_all.at[shard])
    positive_pair = pair_copy(1, positive_all.at[shard], positive_all.at[shard])
    gate_pair = pair_copy(2, gate_hbm, gate_all.at[shard])
    up_pair = pair_copy(3, up_hbm, up_all.at[shard])
    back_pair = pair_copy(4, back_out.at[other], back_in)
    query_pair.start()
    positive_pair.start()
    each_partner(lambda step: code_copy(step).start())

    stream = residual_ref[...].astype(f32)
    root_inverse = lax.rsqrt(jnp.mean(stream * stream, axis=-1, keepdims=True) + EPSILON)
    gain = gain_ref[...].astype(f32)
    normed = (stream * root_inverse * gain).astype(bf16)
    lane = iota((tokens, 128), 1)
    ids = ids_ref[...]
    units = units_ref[...].astype(f32)
    first = (ids[:, 0:1] == lane).astype(f32)
    second = (ids[:, 1:2] == lane).astype(f32)
    taken = first + second
    share = first * units[:, 0:1] + second * units[:, 1:2]
    before = (iota((tokens, tokens), 1) < iota((tokens, tokens), 0)).astype(bf16)
    rank = matmul(before, taken.astype(bf16))
    spread_lane = iota((128, owners * block), 1)
    spread = (spread_lane // block == iota((128, owners * block), 0)).astype(bf16)
    wide_taken = matmul(taken.astype(bf16), spread)
    wide_rank = matmul(rank.astype(bf16), spread)
    wide_share = matmul(share.astype(bf16), spread)
    place = iota((tokens, owners * block), 1) % block
    slot_hit = jnp.where(
        (wide_taken > 0.5) & (wide_rank == (place % slots).astype(f32)), 1.0, 0.0
    )
    low = jnp.where(place < slots, slot_hit, 0.0)
    high = slot_hit - low
    select = jnp.concatenate([low, high], axis=0)
    weighted = select * jnp.concatenate([wide_share, wide_share], axis=0) * (1.0 / 256.0)
    combine[...] = weighted.astype(bf16)
    pick = select.T.astype(bf16)
    stacked = jnp.concatenate([normed[:, :half], normed[:, half:]], axis=0)
    for tile in range(0, half, 256):
        rows = matmul(pick, stacked[:, tile : tile + 256]).astype(bf16)
        rows_out[:, :, tile : tile + 256] = rows.reshape(owners, block, 256)

    place_t = iota((tokens, 128), 0)
    file_place = iota((tokens, files), 1)
    token_row = iota((tokens, files), 0)
    inverse = jnp.zeros((tokens, 1), f32)
    member = jnp.zeros((tokens, 128), f32)
    member_all = jnp.zeros((tokens, files), f32)
    end = 0
    for file in range(file_count):
        length = lengths_ref[0, file]
        start, end = end, end + length
        inside = (place_t >= start) & (place_t < end)
        member = jnp.where(inside & (lane == me * file_count + file), 1.0, member)
        inside_all = (token_row >= start) & (token_row < end)
        owned = (me * 2 + shard) * file_count + file
        member_all = jnp.where(inside_all & (file_place == owned), 1.0, member_all)
        length_row = jnp.zeros((tokens, 1), f32) + length.astype(f32)
        row_id = iota((tokens, 1), 0)
        inverse = jnp.where((row_id >= start) & (row_id < end), 1.0 / length_row, inverse)
    spread_meta = (
        iota((128, owners * slots), 1) // slots == iota((128, owners * slots), 0)
    ).astype(bf16)
    meta_taken = matmul(taken.astype(bf16), spread_meta)
    meta_rank = matmul(rank.astype(bf16), spread_meta)
    meta_slot = (iota((tokens, owners * slots), 1) % slots).astype(f32)
    meta_hit = jnp.where((meta_taken > 0.5) & (meta_rank == meta_slot), 1.0, 0.0).T
    meta_hit = meta_hit.astype(bf16)
    slot_inverse = jnp.dot(
        meta_hit.astype(f32),
        jnp.broadcast_to(inverse, (tokens, 128)),
        precision=lax.Precision.HIGHEST,
        preferred_element_type=f32,
    )
    meta = matmul(meta_hit, member.astype(bf16)) * slot_inverse
    meta_out[...] = meta.reshape(owners, slots, 128)

    rows_in[me] = rows_out[me]
    meta_in[me] = meta_out[me]
    each_partner(lambda step: meta_copy(step).start())
    each_partner(lambda step: rows_copy(step).start())
    gate_pair.start()
    up_pair.start()

    query_pair.wait()
    positive_pair.wait()
    each_partner(lambda step: code_copy(step).wait())
    queries = query_all[...].reshape(files, width)
    codes = code_all[...].reshape(files, width)
    scores = matmul_t(codes, queries) * SCORE_SCALE
    top = jnp.max(scores, axis=0, keepdims=True)
    exponent = jnp.exp(scores - top)
    probabilities = exponent / jnp.sum(exponent, axis=0, keepdims=True)
    positives = jnp.concatenate([positive_all[0, 0:1], positive_all[1, 0:1]], axis=1)
    onehot = (iota((files, files), 0) == positives).astype(f32)
    weights = (GRAD_SCALE * (probabilities - onehot)).astype(bf16)
    own = pl.ds(pl.multiple_of(shard * half, half), half)
    half_queries = query_all[:, :, own].reshape(files, half)
    code_grad = matmul(weights, half_queries).astype(bf16)
    local_down.wait()
    for tile in range(0, ff, 256):
        part = matmul(code_grad, down_own[:, tile : tile + 256])
        part = part.reshape(owners, 2, file_count, 256)
        for side in range(2):
            back_out[side, :, tile : tile + 256] = part[:, side].reshape(
                owners * file_count, 256
            )
    back_pair.start()
    token_weights = matmul(member_all.astype(bf16), weights).astype(bf16)
    token_cot = (matmul(token_weights, queries) * inverse).astype(bf16)

    each_partner(lambda step: meta_copy(step).wait())
    each_partner(lambda step: rows_copy(step).wait())
    rows_f32 = rows_in[...].astype(f32)
    for side in range(2):
        rows_expert[side] = (
            rows_f32[:, side * slots : (side + 1) * slots].reshape(owners * slots, half)
        ).astype(bf16)
    back_pair.wait()
    back_total[...] = (back_out[shard] + back_in[...]).astype(bf16)
    meta_rows = meta_in[...].reshape(owners * slots, 128)
    chosen = jnp.where(meta_rows > 0.0, 1.0, 0.0).astype(bf16)
    chosen_scale = jnp.sum(meta_rows, axis=1, keepdims=True)
    for tile in range(0, ff, 256):
        hidden_back[:, tile : tile + 256] = (
            matmul(chosen[:, : owners * file_count], back_total[:, tile : tile + 256])
            * chosen_scale
        )
    local_gate.wait()
    local_up.wait()
    gate_pair.wait()
    up_pair.wait()

    def hidden_tile(tile, carry):
        where = pl.ds(pl.multiple_of(tile * 256, 256), 256)
        gate_pre = matmul(rows_expert[0], gate_all[0, :, where]) + matmul(
            rows_expert[1], gate_all[1, :, where]
        )
        up_pre = matmul(rows_expert[0], up_all[0, :, where]) + matmul(
            rows_expert[1], up_all[1, :, where]
        )
        back_hidden = hidden_back[:, where]
        sigmoid_gate = jax.nn.sigmoid(gate_pre)
        grad_hidden[0, :, where] = (
            back_hidden * up_pre * sigmoid_gate * (1.0 + gate_pre * (1.0 - sigmoid_gate))
        ).astype(bf16)
        grad_hidden[1, :, where] = (back_hidden * gate_pre * sigmoid_gate).astype(bf16)
        return carry

    lax.fori_loop(0, ff // 256, hidden_tile, 0)

    def grad_tile(tile, carry):
        where = pl.ds(pl.multiple_of(tile * 256, 256), 256)
        sides = []
        for side in range(2):
            part = matmul_t(grad_hidden[0], gate_all[side, where, :]) + matmul_t(
                grad_hidden[1], up_all[side, where, :]
            )
            sides.append(part.reshape(owners, slots, 256))
        grads_out[:, :, where] = jnp.concatenate(sides, axis=1).astype(bf16)
        return carry

    lax.fori_loop(0, half // 256, grad_tile, 0)

    grads_in[me] = grads_out[me]
    each_partner(lambda step: grads_copy(step).start())
    each_partner(lambda step: grads_copy(step).wait())

    picked = grads_in[...].reshape(owners * block, half)
    summed = matmul(combine[...], picked)
    normed_grad = jnp.concatenate([summed[:tokens], summed[tokens:]], axis=1)
    scaled = gain * normed_grad
    correction = jnp.mean(scaled * stream, axis=-1, keepdims=True)
    out_ref[...] = (
        token_cot.astype(f32)
        + root_inverse * scaled
        - stream * (root_inverse * root_inverse * root_inverse) * correction
    ).astype(bf16)


def per_device(
    mesh,
    query_reps,
    code_reps,
    positives,
    file_lengths,
    residual,
    norm_gain,
    expert_ids,
    gate_units,
    w_gate,
    w_up,
    w_down,
):
    owners = mesh.shape["expert"]
    columns, width = code_reps.shape
    files = owners * columns
    tokens = residual.shape[1]
    picks = expert_ids.shape[2]
    file_count = file_lengths.shape[2]
    ff = w_gate.shape[2]
    slots = 3 * tokens * picks // (2 * owners)
    fits = (
        mesh.shape["dp"] == 2
        and picks == 2
        and files <= 256
        and tokens == 128
        and owners * file_count <= 128
        and slots % 8 == 0
        and width % 512 == 0
        and ff % 256 == 0
    )
    if not fits:
        return collective_plan(
            query_reps,
            code_reps,
            positives,
            file_lengths,
            residual,
            norm_gain,
            expert_ids,
            gate_units,
            w_gate,
            w_up,
            w_down,
        )
    half = width // 2
    block = 2 * slots
    bf16, f32 = jnp.bfloat16, jnp.float32
    vmem = pl.BlockSpec(memory_space=pltpu.VMEM)
    hbm = pl.BlockSpec(memory_space=pl.ANY)
    dma = pltpu.SemaphoreType.DMA
    result = pl.pallas_call(
        functools.partial(fused_kernel, owners),
        out_shape=jax.ShapeDtypeStruct((tokens, width), bf16),
        in_specs=[pl.BlockSpec(memory_space=pltpu.SMEM)] + [vmem] * 7 + [hbm] * 3,
        out_specs=vmem,
        scratch_shapes=[
            pltpu.VMEM((2, files // 2, width), bf16),
            pltpu.VMEM((owners, columns, width), bf16),
            pltpu.VMEM((2, 8, files // 2), jnp.int32),
            pltpu.VMEM((2, half, ff), bf16),
            pltpu.VMEM((2, half, ff), bf16),
            pltpu.VMEM((half, ff), bf16),
            pltpu.VMEM((owners, block, half), bf16),
            pltpu.VMEM((owners, block, half), bf16),
            pltpu.VMEM((owners, slots, 128), f32),
            pltpu.VMEM((owners, slots, 128), f32),
            pltpu.VMEM((2, files // 2, ff), f32),
            pltpu.VMEM((files // 2, ff), f32),
            pltpu.VMEM((files // 2, ff), bf16),
            pltpu.VMEM((2, owners * slots, half), bf16),
            pltpu.VMEM((owners * slots, ff), f32),
            pltpu.VMEM((2, owners * slots, ff), bf16),
            pltpu.VMEM((owners, block, half), bf16),
            pltpu.VMEM((owners, block, half), bf16),
            pltpu.VMEM((2 * tokens, owners * block), bf16),
            dma((3,)),
            dma((5,)),
            dma((5,)),
        ]
        + [dma((owners,))] * 8,
        compiler_params=pltpu.CompilerParams(
            collective_id=0, has_side_effects=True, vmem_limit_bytes=52 * 1024 * 1024
        ),
        cost_estimate=pl.CostEstimate(
            flops=5 * 10**9, bytes_accessed=6 * 10**6, transcendentals=10**6
        ),
    )(
        file_lengths[0],
        query_reps,
        code_reps,
        positives[None],
        residual[0],
        norm_gain[None],
        expert_ids[0],
        gate_units[0],
        w_gate[0],
        w_up[0],
        w_down[0],
    )
    return result[None]


def solution(mesh):
    return jax.shard_map(
        functools.partial(per_device, mesh),
        mesh=mesh,
        in_specs=(
            P("dp", None),
            P("expert", None),
            P("dp"),
            P("expert", "dp", None),
            P("expert", "dp", None),
            P(),
            P("expert", "dp", None),
            P("expert", "dp", None),
            P("expert", "dp", None),
            P("expert", "dp", None),
            P("expert", "dp", None),
        ),
        out_specs=P("expert", "dp", None),
        check_vma=False,
    )
```
